128 devices in a mesh: freq: 8 (over x, y_lo), mat: 16 (over z, y_hi, core).
Axes of the slice: x: 4, y: 4 (y_hi: 2, y_lo: 2; y = y_hi * 2 + y_lo), z: 4, core: 2. Of those that a mesh axis runs over, the one named last changes fastest.
Arguments:
- traces: bfloat16 [2048, 64, 4096], P('freq', None, 'mat'), may hold values from -6 to 6
- reflection: bfloat16 [16, 2, 4096, 4096], P('freq', None, 'mat'), may hold values from -0.0625 to 0.0625
- onset: int32 [64, 4096], P(None, 'mat'), may hold values from 512 to 2047
Outputs:
- windowed: bfloat16 [2048, 64, 4096], P('freq', None, 'mat')
The draws below stay inside these ranges and needn't reach their ends.
Inputs may be any that keep to these rules, and one draw needn't show every extreme that they name: onset sample of the direct arrival for each focal point and receiver.
All inputs are finite; a program needn't handle non-finite values.
Results may differ from the reference program's by a relative error of at most 0.0069.
Values may be sent and summed in bfloat16 or wider, within the bound.
A program may use at most 128 MiB of HBM per device.

```python
import math
import jax
import jax.numpy as jnp
from jax import lax

NR = 4096
NT = 2048
P_SIZE = 64
NF = 16
N_FREQ = 8


def plant(array, key, smallest, top_value):
    spot = [jax.random.randint(jax.random.fold_in(key, axis), (), 0, length) for axis, length in enumerate(array.shape)]
    widest = array.shape.index(max(array.shape))
    neighbour = spot[:widest] + [(spot[widest] + 1) % array.shape[widest]] + spot[widest + 1:]
    return array.at[tuple(spot)].set(smallest).at[tuple(neighbour)].set(top_value)


def steps_of(own_key, shape, shards, low, largest):
    loudness, own = 1.0, jax.random.fold_in(own_key, 6)
    for dim, shards_of in shards:
        draws = jnp.exp(jax.random.uniform(jax.random.fold_in(own, dim), (shards_of,), jnp.float32, low / len(shards), largest / len(shards)))
        loudness = loudness * jnp.repeat(draws, shape[dim] // shards_of).reshape([-1 if axis == dim else 1 for axis in range(len(shape))])
    return loudness


def bell_draw(own_key, dims, deviation, most, shards=(), kind=jnp.bfloat16):
    values = deviation * jax.random.normal(own_key, dims, jnp.float32)
    if shards:
        values = values * steps_of(own_key, dims, shards, -0.22, 0.18)
    return jnp.clip(values, -most, most).astype(kind)


def setup_inputs(seed: int = 0) -> dict:
    key_of = jax.random.split(jax.random.key(seed), 4)
    traces = bell_draw(key_of[0], (NT, P_SIZE, NR), 1.0, 6.0, ((0, 8), (2, 16)))
    reflection = bell_draw(key_of[1], (NF, 2, NR, NR), (2 * NR) ** -0.5, 0.0625, ((0, 8), (2, 16)))
    onset = plant(jax.random.randint(key_of[2], (P_SIZE, NR), NT // 4, NT), jax.random.fold_in(key_of[2], 1), NT // 4, NT - 1).astype(jnp.int32)
    return dict(traces=traces, reflection=reflection, onset=onset)


def forward_table(base_band, first_band, band_count, earliest_sample_time, sample_time_count, sampling_interval):
    angular_freq_list = base_band + first_band + jnp.arange(band_count, dtype=jnp.int32)
    sample_moments = earliest_sample_time + jnp.arange(sample_time_count, dtype=jnp.int32)
    phase_angles = (angular_freq_list[:, None] * sample_moments[None, :] % sampling_interval).astype(jnp.float32) * (2.0 * math.pi / sampling_interval)
    factor = 1.0 / math.sqrt(sampling_interval)
    table = jnp.stack([jnp.cos(phase_angles) * factor, -jnp.sin(phase_angles) * factor], axis=1)
    return table.reshape(2 * band_count, sample_time_count).astype(jnp.bfloat16)

def inverse_table(base_band, first_band, band_count, earliest_sample_time, sample_time_count, sampling_interval, bands_total):
    angular_freq_list = base_band + first_band + jnp.arange(band_count, dtype=jnp.int32)
    sample_moments = earliest_sample_time + jnp.arange(sample_time_count, dtype=jnp.int32)
    phase_angles = (sample_moments[:, None] * angular_freq_list[None, :] % sampling_interval).astype(jnp.float32) * (2.0 * math.pi / sampling_interval)
    factor = 1.0 / math.sqrt(bands_total)
    table = jnp.stack([jnp.cos(phase_angles) * factor, -jnp.sin(phase_angles) * factor], axis=2)
    return table.reshape(sample_time_count, 2 * band_count).astype(jnp.bfloat16)

def reference(traces, reflection, onset):
    base_band = NT // 16
    forward = forward_table(base_band, 0, NF, 0, NT, NT)
    spectra = jnp.dot(forward, traces.reshape(NT, P_SIZE * NR), preferred_element_type=jnp.float32)
    spectra = spectra.astype(jnp.bfloat16).reshape(NF, 2, P_SIZE, NR)

    def respond(operands):
        spectrum, matrix = operands
        product = jnp.dot(spectrum.reshape(2 * P_SIZE, NR), matrix.reshape(2 * NR, NR).T, preferred_element_type=jnp.float32)
        product = product.reshape(2, P_SIZE, 2, NR)
        return jnp.stack([product[0, :, 0] - product[1, :, 1], product[1, :, 0] + product[0, :, 1]]).astype(jnp.bfloat16)
    response = lax.map(respond, (spectra, reflection))
    response_rows = response.reshape(2 * NF, P_SIZE * NR)
    tile_row_group = NT // N_FREQ

    def window(block_index):
        earliest_sample_time = block_index * tile_row_group
        inverse = inverse_table(base_band, 0, NF, earliest_sample_time, tile_row_group, NT, NF)
        wavelet_trace = jnp.dot(inverse, response_rows, preferred_element_type=jnp.float32).reshape(tile_row_group, P_SIZE, NR)
        sample_moments = earliest_sample_time + jnp.arange(tile_row_group, dtype=jnp.int32)
        return jnp.where(sample_moments[:, None, None] < onset[None], wavelet_trace, 0.0).astype(jnp.bfloat16)
    windowed = lax.map(window, jnp.arange(N_FREQ, dtype=jnp.int32))
    return windowed.reshape(NT, P_SIZE, NR)
```

```python
import math

import jax
import jax.numpy as jnp
from jax import lax
from jax.sharding import PartitionSpec as P


def forward_table(
    base_band, first_band, band_count, earliest_sample_time, sample_time_count, sampling_interval
):
    angular_freq_list = base_band + first_band + jnp.arange(band_count, dtype=jnp.int32)
    sample_moments = earliest_sample_time + jnp.arange(sample_time_count, dtype=jnp.int32)
    phase_angles = (
        angular_freq_list[:, None] * sample_moments[None, :] % sampling_interval
    ).astype(jnp.float32) * (2.0 * math.pi / sampling_interval)
    factor = 1.0 / math.sqrt(sampling_interval)
    table = jnp.stack([jnp.cos(phase_angles) * factor, -jnp.sin(phase_angles) * factor], axis=1)
    return table.reshape(2 * band_count, sample_time_count).astype(jnp.bfloat16)


def inverse_table(
    base_band,
    first_band,
    band_count,
    earliest_sample_time,
    sample_time_count,
    sampling_interval,
    bands_total,
):
    angular_freq_list = base_band + first_band + jnp.arange(band_count, dtype=jnp.int32)
    sample_moments = earliest_sample_time + jnp.arange(sample_time_count, dtype=jnp.int32)
    phase_angles = (
        sample_moments[:, None] * angular_freq_list[None, :] % sampling_interval
    ).astype(jnp.float32) * (2.0 * math.pi / sampling_interval)
    factor = 1.0 / math.sqrt(bands_total)
    table = jnp.stack([jnp.cos(phase_angles) * factor, -jnp.sin(phase_angles) * factor], axis=2)
    return table.reshape(sample_time_count, 2 * band_count).astype(jnp.bfloat16)


def accumulate(reflection, panels):
    return jnp.einsum("kcpw,kdrw->kcpdr", panels, reflection, preferred_element_type=jnp.float32)


def on_device(traces, reflection, onset):
    temporal_rows, focal_count, recv_rows = traces.shape
    freq_devices = lax.axis_size("freq")
    sampling_interval = temporal_rows * freq_devices
    per_device = reflection.shape[0]
    bands_total = per_device * freq_devices
    base_band = sampling_interval // 16
    earliest_sample_time = lax.axis_index("freq") * temporal_rows
    earliest = lax.axis_index("freq") * temporal_rows
    forward = forward_table(
        base_band, 0, bands_total, earliest, temporal_rows, sampling_interval
    )
    partial = jnp.dot(
        forward, traces.reshape(temporal_rows, -1), preferred_element_type=jnp.float32
    )
    partial = partial.astype(jnp.bfloat16).reshape(
        freq_devices, per_device, 2, focal_count, recv_rows
    )
    parts = lax.all_to_all(partial, "freq", split_axis=0, concat_axis=0, tiled=True)
    spectra = jnp.sum(parts.astype(jnp.float32), axis=0).astype(jnp.bfloat16)
    products = accumulate(reflection, lax.all_gather(spectra, "mat", axis=3, tiled=True))
    real_part = products[:, 0, :, 0] - products[:, 1, :, 1]
    imag_part = products[:, 1, :, 0] + products[:, 0, :, 1]
    response = jnp.stack([real_part, imag_part], axis=1).astype(jnp.bfloat16)
    pieces = lax.all_gather(response, "freq", axis=0, tiled=True)
    piece_bands = pieces.shape[0]
    table = inverse_table(
        base_band,
        jnp.int32(0),
        piece_bands,
        earliest_sample_time,
        temporal_rows,
        sampling_interval,
        bands_total,
    )
    wavelet_trace = jnp.dot(
        table, pieces.reshape(2 * piece_bands, -1), preferred_element_type=jnp.float32
    )
    wavelet_trace = wavelet_trace.reshape(temporal_rows, focal_count, recv_rows)
    sample_moments = earliest_sample_time + jnp.arange(temporal_rows, dtype=jnp.int32)
    return jnp.where(sample_moments[:, None, None] < onset[None], wavelet_trace, 0.0).astype(
        jnp.bfloat16
    )


def solution(mesh):
    placed = (P("freq", None, "mat"), P("freq", None, "mat", None), P(None, "mat"))
    return jax.shard_map(
        on_device, mesh=mesh, in_specs=placed, out_specs=P("freq", None, "mat"), check_vma=False
    )
```

```python
import math

import jax
import jax.numpy as jnp
from jax import lax
from jax.experimental import pallas as pl
from jax.experimental.pallas import tpu as pltpu
from jax.sharding import PartitionSpec as P

MESH = pl.DeviceIdType.MESH
HALVES = 2
GROUP = 8
OFFSETS = ((1, 0), (3, 0), (0, 1), (1, 1), (3, 1), (2, 0), (2, 1))


def phases(base_band, band_count, earliest, count, interval):
    bands = base_band + jnp.arange(band_count, dtype=jnp.int32)
    times = earliest + jnp.arange(count, dtype=jnp.int32)
    return (bands[:, None] * times[None, :] % interval).astype(jnp.float32) * (
        2.0 * math.pi / interval
    )


def tables(base_band, band_count, earliest, count, interval):
    angles = phases(base_band, band_count, earliest, count, interval)
    both = jnp.stack([jnp.cos(angles), -jnp.sin(angles)], axis=1).reshape(2 * band_count, count)
    forward = (both * (1.0 / math.sqrt(interval))).astype(jnp.bfloat16)
    inverse = (both * (1.0 / math.sqrt(band_count))).astype(jnp.bfloat16)
    return forward, inverse.T


def spread(table, lanes):
    rows, inner = table.shape
    col = lax.broadcasted_iota(jnp.int32, (inner, lanes), 1) >> 3
    row = lax.broadcasted_iota(jnp.int32, (inner, lanes), 0)
    pick = jnp.where(col == row, 1.0, 0.0).astype(jnp.bfloat16)
    wide = jnp.dot(table, pick, preferred_element_type=jnp.float32)
    sub = lax.broadcasted_iota(jnp.int32, (1, GROUP, lanes), 1)
    lane = lax.broadcasted_iota(jnp.int32, (1, GROUP, lanes), 2) & (GROUP - 1)
    full = jnp.where(sub == lane, wide[:, None, :], 0.0)
    return full.reshape(rows * GROUP, lanes).astype(jnp.bfloat16)


def exchange_kernel(
    traces, reflection, forward, inverse, pieces, inv_out,
    samples, matrix, fwd_wide, inv_wide, partial, parts, spectra, acc, response,
    load_sem, mat_sem, inv_sem, own_sem,
    rs_send, rs_recv, ag_send, ag_recv, fw_send, core_recv, br_send, br_recv,
):
    f = lax.axis_index("freq")
    m = lax.axis_index("mat")
    x, yl = f // 2, f % 2
    z, yh, core = m // 4, (m // 2) % 2, m % 2

    def freq_peer(dx, dy):
        return lax.rem(x + dx, 4) * 2 + lax.rem(yl + dy, 2)

    def mat_peer(dz, dy):
        return lax.rem(z + dz, 4) * 4 + lax.rem(yh + dy, 2) * 2 + core

    other = m + 1 - 2 * core

    barrier = pltpu.get_barrier_semaphore()
    for o in OFFSETS:
        pl.semaphore_signal(barrier, inc=1, device_id=(freq_peer(*o), m), device_id_type=MESH)
        pl.semaphore_signal(barrier, inc=1, device_id=(f, mat_peer(*o)), device_id_type=MESH)
    pl.semaphore_signal(barrier, inc=1, device_id=(f, other), device_id_type=MESH)

    groups = samples.shape[0]
    per_half = groups // HALVES
    times = traces.shape[0]
    width = traces.shape[2]

    def load(g):
        return pltpu.make_async_copy(
            traces.at[:, pl.ds(pl.multiple_of(g * GROUP, GROUP), GROUP), :],
            samples.at[g],
            load_sem.at[g],
        )

    for g in range(groups):
        load(g).start()
    mat_load = pltpu.make_async_copy(reflection, matrix, mat_sem)
    mat_load.start()

    fwd_wide[...] = spread(forward[...], times * GROUP)

    def transform(h):
        def one(i, _):
            g = h * per_half + i
            load(g).wait()
            out = jnp.dot(
                fwd_wide[...],
                samples.at[g].reshape(times * GROUP, width)[...],
                preferred_element_type=jnp.float32,
            )
            out = out.reshape(8, 4, GROUP, width).astype(jnp.bfloat16)
            partial[h, :, :, i] = out
            return 0

        lax.fori_loop(0, per_half, one, 0)

    def rs_copy(h, j):
        to = freq_peer(*OFFSETS[j])
        return pltpu.make_async_remote_copy(
            src_ref=partial.at[h, to], dst_ref=parts.at[h, j],
            send_sem=rs_send.at[h, j], recv_sem=rs_recv.at[h, j],
            device_id=(to, m), device_id_type=MESH,
        )

    def ag_copy(h, j):
        return pltpu.make_async_remote_copy(
            src_ref=spectra.at[h, m], dst_ref=spectra.at[h, m],
            send_sem=ag_send.at[h, j], recv_sem=ag_recv.at[h, j],
            device_id=(f, mat_peer(*OFFSETS[j])), device_id_type=MESH,
        )

    def core_copy(h, j, block):
        return pltpu.make_async_remote_copy(
            src_ref=spectra.at[h, block], dst_ref=spectra.at[h, block],
            send_sem=fw_send.at[h, j], recv_sem=core_recv.at[h, j],
            device_id=(f, other), device_id_type=MESH,
        )

    def br_copy(h, j):
        return pltpu.make_async_remote_copy(
            src_ref=response.at[h], dst_ref=pieces.at[h, f],
            send_sem=br_send.at[h, j], recv_sem=br_recv.at[h, j],
            device_id=(freq_peer(*OFFSETS[j]), m), device_id_type=MESH,
        )

    peers = range(len(OFFSETS))
    last = len(OFFSETS)

    for h in range(HALVES):
        transform(h)
        if h == 0:
            pl.semaphore_wait(barrier, 2 * len(OFFSETS) + 1)
        for j in peers:
            rs_copy(h, j).start()

    inv_wide[...] = spread(inverse[...], inv_wide.shape[1])
    inv_copy = pltpu.make_async_copy(inv_wide, inv_out, inv_sem)
    inv_copy.start()

    for h in range(HALVES):
        total = partial[h, f].astype(jnp.float32)
        for j in peers:
            rs_copy(h, j).wait_recv()
            total = total + parts[h, j].astype(jnp.float32)
        spectra[h, m] = total.astype(jnp.bfloat16)
        for j in peers:
            ag_copy(h, j).start()
        core_copy(h, last, m).start()

    mat_load.wait()
    bands = matrix.shape[0]
    half_rows = per_half * GROUP
    recv_rows = matrix.shape[2]

    def multiply(h, block, first):
        for k in range(bands):
            panel = spectra.at[h, block, pl.ds(2 * k, 2)].reshape(2 * half_rows, width)[...]
            cols = pl.ds(pl.multiple_of(block * width, width), width)
            tile = matrix[k, :, :, cols].reshape(2 * recv_rows, width)
            out = lax.dot_general(
                panel, tile, (((1,), (1,)), ((), ())), preferred_element_type=jnp.float32
            )
            if first:
                acc[k] = out
            else:
                acc[k] += out

    for h in range(HALVES):
        multiply(h, m, True)
        core_copy(h, last, m).wait_recv()
        multiply(h, other, False)
        for j in peers:
            block = mat_peer(*OFFSETS[j])
            ag_copy(h, j).wait_recv()
            core_copy(h, j, source(h, j, mat_peer)).start()
            multiply(h, source(h, j, mat_peer), False)
            core_copy(h, j, m).wait_recv()
            multiply(h, source(h, j, mat_peer) + 1 - 2 * core, False)
        for k in range(bands):
            a = acc[k]
            real = a[:half_rows, :recv_rows] - a[half_rows:, recv_rows:]
            imag = a[half_rows:, :recv_rows] + a[:half_rows, recv_rows:]
            response[h, 2 * k] = real.reshape(per_half, GROUP, width).astype(jnp.bfloat16)
            response[h, 2 * k + 1] = imag.reshape(per_half, GROUP, width).astype(jnp.bfloat16)
        for j in peers:
            br_copy(h, j).start()
        pltpu.make_async_copy(response.at[h], pieces.at[h, f], own_sem.at[h]).start()

    for h in range(HALVES):
        for j in peers:
            br_copy(h, j).wait_recv()
        pltpu.make_async_copy(response.at[h], pieces.at[h, f], own_sem.at[h]).wait()
    for h in range(HALVES):
        for j in peers:
            rs_copy(h, j).wait_send()
            ag_copy(h, j).wait_send()
            core_copy(h, j, m).wait_send()
            br_copy(h, j).wait_send()
        core_copy(h, last, m).wait_send()
    inv_copy.wait()


def source(h, j, mat_peer):
    dz, dy = OFFSETS[j]
    return mat_peer((4 - dz) % 4, dy)


def window_kernel(table, pieces, onset, out):
    times = out.shape[0]
    width = out.shape[2]
    step = 32
    rows = pieces[...].astype(jnp.float32).reshape(table.shape[1], width).astype(jnp.bfloat16)
    left = onset[...] - lax.axis_index("freq") * times
    at = lax.broadcasted_iota(jnp.int32, (step, GROUP, width), 0)

    def one(i, _):
        t = pl.multiple_of(i * step, step)
        signal = jnp.dot(
            table[pl.ds(pl.multiple_of(i * step * GROUP, step * GROUP), step * GROUP), :],
            rows,
            preferred_element_type=jnp.float32,
        ).reshape(step, GROUP, width)
        kept = jnp.where(at < (left - t)[None], signal, 0.0)
        out[pl.ds(t, step)] = kept.astype(jnp.bfloat16)
        return 0

    lax.fori_loop(0, times // step, one, 0, unroll=2)


def on_device(traces, reflection, onset):
    times, focal, width = traces.shape
    devices = lax.axis_size("freq")
    mats = lax.axis_size("mat")
    interval = times * devices
    per_device = reflection.shape[0]
    bands = per_device * devices
    rows = 2 * per_device
    half = focal // HALVES
    per_half = half // GROUP
    peers = len(OFFSETS)
    forward, inverse = tables(
        interval // 16, bands, lax.axis_index("freq") * times, times, interval
    )
    bf16 = jnp.bfloat16
    dma = pltpu.SemaphoreType.DMA
    anywhere = pl.BlockSpec(memory_space=pl.ANY)
    vmem = pl.BlockSpec(memory_space=pltpu.VMEM)
    pieces, table = pl.pallas_call(
        exchange_kernel,
        out_shape=(
            jax.ShapeDtypeStruct((HALVES, devices, rows, per_half, GROUP, width), bf16),
            jax.ShapeDtypeStruct((times * GROUP, 2 * bands * GROUP), bf16),
        ),
        in_specs=[anywhere, anywhere, vmem, vmem],
        out_specs=(anywhere, anywhere),
        scratch_shapes=[
            pltpu.VMEM((focal // GROUP, times, GROUP, width), bf16),
            pltpu.VMEM(reflection.shape, bf16),
            pltpu.VMEM((2 * bands * GROUP, times * GROUP), bf16),
            pltpu.VMEM((times * GROUP, 2 * bands * GROUP), bf16),
            pltpu.VMEM((HALVES, devices, rows, per_half, GROUP, width), bf16),
            pltpu.VMEM((HALVES, peers, rows, per_half, GROUP, width), bf16),
            pltpu.VMEM((HALVES, mats, rows, per_half, GROUP, width), bf16),
            pltpu.VMEM((per_device, 2 * half, 2 * width), jnp.float32),
            pltpu.VMEM((HALVES, rows, per_half, GROUP, width), bf16),
            dma((focal // GROUP,)),
            dma,
            dma,
            dma((HALVES,)),
            dma((HALVES, peers)),
            dma((HALVES, peers)),
            dma((HALVES, peers)),
            dma((HALVES, peers)),
            dma((HALVES, peers + 1)),
            dma((HALVES, peers + 1)),
            dma((HALVES, peers)),
            dma((HALVES, peers)),
        ],
        compiler_params=pltpu.CompilerParams(
            collective_id=0, has_side_effects=True, vmem_limit_bytes=60 * 2**20
        ),
        name="exchange",
    )(traces, reflection, forward, inverse)
    return pl.pallas_call(
        window_kernel,
        grid=(focal // GROUP,),
        out_shape=jax.ShapeDtypeStruct((times, focal, width), bf16),
        in_specs=[
            pl.BlockSpec(table.shape, lambda g: (0, 0)),
            pl.BlockSpec(
                (None, devices, rows, None, GROUP, width),
                lambda g: (g // per_half, 0, 0, g % per_half, 0, 0),
            ),
            pl.BlockSpec((GROUP, width), lambda g: (g, 0)),
        ],
        out_specs=pl.BlockSpec((times, GROUP, width), lambda g: (0, g, 0)),
        compiler_params=pltpu.CompilerParams(vmem_limit_bytes=60 * 2**20),
        name="window",
    )(table, pieces, onset)


def solution(mesh):
    placed = (P("freq", None, "mat"), P("freq", None, "mat", None), P(None, "mat"))
    return jax.shard_map(
        on_device, mesh=mesh, in_specs=placed, out_specs=P("freq", None, "mat"), check_vma=False
    )
```

```python
import math

import jax
import jax.numpy as jnp
from jax import lax
from jax.experimental import pallas as pl
from jax.experimental.pallas import tpu as pltpu
from jax.sharding import PartitionSpec as P

MESH = pl.DeviceIdType.MESH
HALVES = 4
GROUP = 8
STEPS = 4
LEAD, SPACING = (-6.0, 0.0, 3.8, 5.0, 8.0), 9.6
OFFSETS = ((0, 1), (1, 0), (3, 0), (2, 0), (1, 1), (3, 1), (2, 1))
ACROSS, DIRECT, RELAYED = 0, (0, 1, 2, 3), (4, 5, 6)


def table_pair(first, bands, times, interval):
    k = first + lax.broadcasted_iota(jnp.int32, (bands, times), 0)
    t = lax.axis_index("freq") * times + lax.broadcasted_iota(jnp.int32, (bands, times), 1)
    angles = ((k * t) & (interval - 1)).astype(jnp.float32) * (2.0 * math.pi / interval)
    return jnp.cos(angles), -jnp.sin(angles)


def kron_rows(wide):
    rows, lanes = wide.shape
    sub = lax.broadcasted_iota(jnp.int32, (1, GROUP, lanes), 1)
    lane = lax.broadcasted_iota(jnp.int32, (1, GROUP, lanes), 2) & (GROUP - 1)
    full = jnp.where(sub == lane, wide[:, None, :], 0.0)
    return full.reshape(rows * GROUP, lanes).astype(jnp.bfloat16)


def repeat_lanes(inner, lanes):
    col = lax.broadcasted_iota(jnp.int32, (inner, lanes), 1) >> 3
    row = lax.broadcasted_iota(jnp.int32, (inner, lanes), 0)
    return jnp.where(col == row, 1.0, 0.0).astype(jnp.bfloat16)


def exchange_kernel(
    traces, reflection, pieces, inv_out,
    samples, matrix, fwd_wide, inv_wide, partial, parts, spectra, acc, response,
    load_sem, mat_sem, inv_sem, own_sem,
    rs_send, rs_recv, ag_send, ag_recv, fw_send, core_recv, br_send, br_recv,
):
    f = lax.axis_index("freq")
    m = lax.axis_index("mat")
    x, yl = f // 2, f % 2
    z, yh, core = m // 4, (m // 2) % 2, m % 2

    def freq_peer(dx, dy):
        return lax.rem(x + dx, 4) * 2 + lax.rem(yl + dy, 2)

    def mat_peer(dz, dy):
        return lax.rem(z + dz, 4) * 4 + lax.rem(yh + dy, 2) * 2 + core

    def source(j):
        dz, dy = OFFSETS[j]
        return mat_peer((4 - dz) % 4, dy)

    flip = 1 - 2 * core
    other = m + flip
    freq_ids = [freq_peer(*o) for o in OFFSETS]
    mat_ids = [mat_peer(*o) for o in OFFSETS]

    barrier = pltpu.get_barrier_semaphore()
    for o in OFFSETS:
        pl.semaphore_signal(barrier, inc=1, device_id=(freq_peer(*o), m), device_id_type=MESH)
        pl.semaphore_signal(barrier, inc=1, device_id=(f, mat_peer(*o)), device_id_type=MESH)
    pl.semaphore_signal(barrier, inc=1, device_id=(f, other), device_id_type=MESH)

    groups = samples.shape[0]
    per_half = groups // HALVES
    times = traces.shape[0]
    width = traces.shape[2]

    def load(g):
        return pltpu.make_async_copy(
            traces.at[:, pl.ds(pl.multiple_of(g * GROUP, GROUP), GROUP), :],
            samples.at[g],
            load_sem.at[g],
        )

    for g in range(groups):
        load(g).start()
    mat_load = pltpu.make_async_copy(reflection, matrix, mat_sem)

    bands_here = matrix.shape[0]
    owners = partial.shape[1]
    bands = bands_here * owners
    interval = times * owners
    table = jnp.concatenate(table_pair(interval // 16, bands, times, interval), axis=0)
    forward = (table * (1.0 / math.sqrt(interval))).astype(jnp.bfloat16)
    fwd_wide[...] = kron_rows(
        jnp.dot(
            forward, repeat_lanes(times, times * GROUP), preferred_element_type=jnp.float32
        )
    )

    def transform(h):
        def one(i, _):
            g = h * per_half + i
            load(g).wait()
            out = jnp.dot(
                fwd_wide[...],
                samples.at[g].reshape(times * GROUP, width)[...],
                preferred_element_type=jnp.float32,
            )
            out = out.reshape(2, owners, bands_here, GROUP, width).astype(jnp.bfloat16)
            partial[h, :, :, 0, i] = out[0]
            partial[h, :, :, 1, i] = out[1]
            return 0

        lax.fori_loop(0, per_half, one, 0)

    def rs_copy(h, j):
        to = freq_ids[j]
        return pltpu.make_async_remote_copy(
            src_ref=partial.at[h, to], dst_ref=parts.at[h, j],
            send_sem=rs_send.at[h], recv_sem=rs_recv.at[h],
            device_id=(to, m), device_id_type=MESH,
        )

    def rs_all(h):
        return pltpu.make_async_remote_copy(
            src_ref=parts.at[h], dst_ref=parts.at[h],
            send_sem=rs_send.at[h], recv_sem=rs_recv.at[h],
            device_id=(f, other), device_id_type=MESH,
        )

    def ag_copy(h, j):
        relayed = j in RELAYED
        kind = 2 if relayed else int(j != ACROSS)
        return pltpu.make_async_remote_copy(
            src_ref=spectra.at[h, core, (1 + ACROSS) if relayed else 0],
            dst_ref=spectra.at[h, core, 1 + j],
            send_sem=ag_send.at[h, kind], recv_sem=ag_recv.at[h, kind],
            device_id=(f, mat_ids[j - 3] if relayed else mat_ids[j]), device_id_type=MESH,
        )

    def ag_all(h, kind):
        first, count = ((1, 1), (2, 3), (5, 3))[kind]
        part = spectra.at[h, core, pl.ds(first, count)]
        return pltpu.make_async_remote_copy(
            src_ref=part, dst_ref=part,
            send_sem=ag_send.at[h, kind], recv_sem=ag_recv.at[h, kind],
            device_id=(f, other), device_id_type=MESH,
        )

    def core_copy(h, part):
        first, count = ((0, 5), (5, 3))[part]
        held = spectra.at[h, core, pl.ds(first, count)]
        return pltpu.make_async_remote_copy(
            src_ref=held, dst_ref=held,
            send_sem=fw_send.at[h, part], recv_sem=core_recv.at[h, part],
            device_id=(f, other), device_id_type=MESH,
        )

    def br_copy(h, j):
        return pltpu.make_async_remote_copy(
            src_ref=response.at[h], dst_ref=pieces.at[h, f],
            send_sem=br_send.at[h], recv_sem=br_recv.at[h],
            device_id=(freq_ids[j], m), device_id_type=MESH,
        )

    def br_all(h):
        part = pieces.at[h, pl.ds(0, len(OFFSETS))]
        return pltpu.make_async_remote_copy(
            src_ref=part, dst_ref=part,
            send_sem=br_send.at[h], recv_sem=br_recv.at[h],
            device_id=(f, other), device_id_type=MESH,
        )

    peers = range(len(OFFSETS))

    for h in range(HALVES):
        transform(h)
        if h == 0:
            mat_load.start()
            pl.semaphore_wait(barrier, 2 * len(OFFSETS) + 1)
            for j in peers:
                rs_copy(h, j).start()

    inverse = (table * (1.0 / math.sqrt(bands))).astype(jnp.bfloat16)
    inv_wide[...] = kron_rows(
        lax.dot_general(
            inverse,
            repeat_lanes(2 * bands, 2 * bands * GROUP),
            (((0,), (0,)), ((), ())),
            preferred_element_type=jnp.float32,
        )
    )
    inv_copy = pltpu.make_async_copy(inv_wide, inv_out, inv_sem)
    inv_copy.start()

    half_rows = per_half * GROUP
    recv_rows = matrix.shape[2]

    def multiply(h, side, slot):
        block = m if slot == 0 else source(slot - 1)
        block = block + (side - core)
        for k in range(bands_here):
            panel = spectra.at[h, side, slot, k].reshape(2 * half_rows, width)[...]
            cols = pl.ds(pl.multiple_of(block * width, width), width)
            tile = matrix[k, :, :, cols].reshape(2 * recv_rows, width)
            out = lax.dot_general(
                panel, tile, (((1,), (1,)), ((), ())), preferred_element_type=jnp.float32
            )
            if slot == 0 and side is core:
                acc[h, k] = out
            else:
                acc[h, k] += out

    def send_parts(h):
        if h == 0:
            return
        rs_all(h - 1).wait_send()
        for j in peers:
            rs_copy(h, j).start()

    def add_up(h):
        rs_all(h).wait_recv()
        total = partial[h, f].astype(jnp.float32)
        for j in peers:
            total = total + parts[h, j].astype(jnp.float32)
        spectra[h, core, 0] = total.astype(jnp.bfloat16)
        for j in DIRECT:
            ag_copy(h, j).start()

    def relay(h):
        ag_all(h, 0).wait_recv()
        for j in RELAYED:
            ag_copy(h, j).start()

    def first_blocks(h):
        if h == 0:
            mat_load.wait()
        ag_all(h, 1).wait_recv()
        core_copy(h, 0).start()
        for slot in range(5):
            multiply(h, core, slot)

    def last_blocks(h):
        ag_all(h, 2).wait_recv()
        core_copy(h, 1).start()
        for slot in range(5, 8):
            multiply(h, core, slot)
        core_copy(h, 0).wait_recv()
        for slot in range(5):
            multiply(h, 1 - core, slot)
        core_copy(h, 1).wait_recv()
        for slot in range(5, 8):
            multiply(h, 1 - core, slot)
        for k in range(bands_here):
            a = acc[h, k]
            real = a[:half_rows, :recv_rows] - a[half_rows:, recv_rows:]
            imag = a[half_rows:, :recv_rows] + a[:half_rows, recv_rows:]
            response[h, k, 0] = real.reshape(per_half, GROUP, width).astype(jnp.bfloat16)
            response[h, k, 1] = imag.reshape(per_half, GROUP, width).astype(jnp.bfloat16)
        for j in peers:
            br_copy(h, j).start()
        pltpu.make_async_copy(response.at[h], pieces.at[h, f], own_sem.at[h]).start()

    steps = (send_parts, add_up, relay, first_blocks, last_blocks)
    order = sorted(
        (LEAD[i] + h * SPACING / HALVES, i, h) for i in range(len(steps)) for h in range(HALVES)
    )
    for _, i, h in order:
        steps[i](h)

    for h in range(HALVES):
        br_all(h).wait_recv()
        pltpu.make_async_copy(response.at[h], pieces.at[h, f], own_sem.at[h]).wait()
    rs_all(HALVES - 1).wait_send()
    for h in range(HALVES):
        for kind in range(3):
            ag_all(h, kind).wait_send()
        for part in range(2):
            core_copy(h, part).wait_send()
        br_all(h).wait_send()
    inv_copy.wait()


def window_kernel(table, pieces, onset, out, wide, held, left, rows, signal, sems, tab_sem, out_sem):
    times, focal, width = out.shape
    steps = signal.shape[0]
    step = times // steps
    groups = focal // GROUP

    def table_load(i):
        part = pl.ds(i * step * GROUP, step * GROUP)
        return pltpu.make_async_copy(table.at[part], wide.at[part], tab_sem.at[i])

    def store(i):
        return pltpu.make_async_copy(
            signal.at[i], out.at[pl.ds(i * step, step)], out_sem.at[i]
        )

    loads = [pltpu.make_async_copy(pieces.at[h], held.at[h], sems.at[h]) for h in range(HALVES)]
    loads.append(pltpu.make_async_copy(onset, left, sems.at[HALVES]))
    for copy in loads:
        copy.start()
    for i in range(steps):
        table_load(i).start()
    for copy in loads:
        copy.wait()
    per_half = groups // HALVES
    for g in range(groups):
        parts = [
            held[g // per_half, :, :, c, g % per_half]
            .astype(jnp.float32)
            .reshape(wide.shape[1] // 2, width)
            for c in range(2)
        ]
        rows[g] = jnp.concatenate(parts, axis=0).astype(jnp.bfloat16)
    at = lax.axis_index("freq") * times + lax.broadcasted_iota(
        jnp.int32, (step, GROUP, width), 0
    )
    for i in range(steps):
        table_load(i).wait()
        weights = wide[i * step * GROUP : (i + 1) * step * GROUP]
        for g in range(groups):
            value = jnp.dot(weights, rows[g], preferred_element_type=jnp.float32)
            until = left[g * GROUP : (g + 1) * GROUP] - i * step
            kept = jnp.where(at < until[None], value.reshape(step, GROUP, width), 0.0)
            signal[i, :, g * GROUP : (g + 1) * GROUP] = kept.astype(jnp.bfloat16)
        store(i).start()
    for i in range(steps):
        store(i).wait()


def on_device(traces, reflection, onset):
    times, focal, width = traces.shape
    devices = lax.axis_size("freq")
    mats = lax.axis_size("mat")
    per_device = reflection.shape[0]
    bands = per_device * devices
    half = focal // HALVES
    per_half = half // GROUP
    peers = len(OFFSETS)
    bf16 = jnp.bfloat16
    dma = pltpu.SemaphoreType.DMA
    anywhere = pl.BlockSpec(memory_space=pl.ANY)
    pieces, table = pl.pallas_call(
        exchange_kernel,
        out_shape=(
            jax.ShapeDtypeStruct((HALVES, devices, per_device, 2, per_half, GROUP, width), bf16),
            jax.ShapeDtypeStruct((times * GROUP, 2 * bands * GROUP), bf16),
        ),
        in_specs=[anywhere, anywhere],
        out_specs=(anywhere, anywhere),
        scratch_shapes=[
            pltpu.VMEM((focal // GROUP, times, GROUP, width), bf16),
            pltpu.VMEM(reflection.shape, bf16),
            pltpu.VMEM((2 * bands * GROUP, times * GROUP), bf16),
            pltpu.VMEM((times * GROUP, 2 * bands * GROUP), bf16),
            pltpu.VMEM((HALVES, devices, per_device, 2, per_half, GROUP, width), bf16),
            pltpu.VMEM((HALVES, peers, per_device, 2, per_half, GROUP, width), bf16),
            pltpu.VMEM((HALVES, 2, mats // 2, per_device, 2, per_half, GROUP, width), bf16),
            pltpu.VMEM((HALVES, per_device, 2 * half, 2 * width), jnp.float32),
            pltpu.VMEM((HALVES, per_device, 2, per_half, GROUP, width), bf16),
            dma((focal // GROUP,)),
            dma,
            dma,
            dma((HALVES,)),
            dma((HALVES,)),
            dma((HALVES,)),
            dma((HALVES, 3)),
            dma((HALVES, 3)),
            dma((HALVES, 2)),
            dma((HALVES, 2)),
            dma((HALVES,)),
            dma((HALVES,)),
        ],
        compiler_params=pltpu.CompilerParams(
            collective_id=0, has_side_effects=True, vmem_limit_bytes=60 * 2**20
        ),
        name="exchange",
    )(traces, reflection)
    return pl.pallas_call(
        window_kernel,
        out_shape=jax.ShapeDtypeStruct((times, focal, width), bf16),
        in_specs=[anywhere, anywhere, anywhere],
        out_specs=anywhere,
        scratch_shapes=[
            pltpu.VMEM(table.shape, bf16),
            pltpu.VMEM(pieces.shape, bf16),
            pltpu.VMEM(onset.shape, jnp.int32),
            pltpu.VMEM((focal // GROUP, table.shape[1], width), bf16),
            pltpu.VMEM((STEPS, times // STEPS, focal, width), bf16),
            dma((HALVES + 1,)),
            dma((STEPS,)),
            dma((STEPS,)),
        ],
        compiler_params=pltpu.CompilerParams(vmem_limit_bytes=60 * 2**20),
        name="window",
    )(table, pieces, onset)


def solution(mesh):
    placed = (P("freq", None, "mat"), P("freq", None, "mat", None), P(None, "mat"))
    return jax.shard_map(
        on_device, mesh=mesh, in_specs=placed, out_specs=P("freq", None, "mat"), check_vma=False
    )
```

```python
import math

import jax
import jax.numpy as jnp
from jax import lax
from jax.experimental import pallas as pl
from jax.experimental.pallas import tpu as pltpu
from jax.sharding import PartitionSpec as P

MESH = pl.DeviceIdType.MESH
HALVES = 4
GROUP = 8
STEPS = 4
LEAD, SPACING = (-4.5, 0.0, 3.8, 5.0, 8.0), 9.6
OFFSETS = ((0, 1), (1, 0), (3, 0), (2, 0), (1, 1), (3, 1), (2, 1))
ACROSS, DIRECT, RELAYED = 0, (0, 1, 2, 3), (4, 5, 6)


def table_pair(first, bands, times, interval):
    k = first + lax.broadcasted_iota(jnp.int32, (bands, times), 0)
    t = lax.axis_index("freq") * times + lax.broadcasted_iota(jnp.int32, (bands, times), 1)
    angles = ((k * t) & (interval - 1)).astype(jnp.float32) * (2.0 * math.pi / interval)
    return jnp.cos(angles), -jnp.sin(angles)


def kron_rows(wide):
    rows, lanes = wide.shape
    sub = lax.broadcasted_iota(jnp.int32, (1, GROUP, lanes), 1)
    lane = lax.broadcasted_iota(jnp.int32, (1, GROUP, lanes), 2) & (GROUP - 1)
    full = jnp.where(sub == lane, wide[:, None, :], 0.0)
    return full.reshape(rows * GROUP, lanes).astype(jnp.bfloat16)


def repeat_lanes(inner, lanes):
    col = lax.broadcasted_iota(jnp.int32, (inner, lanes), 1) >> 3
    row = lax.broadcasted_iota(jnp.int32, (inner, lanes), 0)
    return jnp.where(col == row, 1.0, 0.0).astype(jnp.bfloat16)


def exchange_kernel(
    traces, reflection, pieces, inv_out,
    samples, matrix, fwd_wide, inv_wide, partial, parts, spectra, acc, response,
    load_sem, mat_sem, inv_sem, own_sem,
    rs_send, rs_recv, ag_send, ag_recv, fw_send, core_recv, br_send, br_recv,
):
    f = lax.axis_index("freq")
    m = lax.axis_index("mat")
    x, yl = f // 2, f % 2
    z, yh, core = m // 4, (m // 2) % 2, m % 2

    def freq_peer(dx, dy):
        return lax.rem(x + dx, 4) * 2 + lax.rem(yl + dy, 2)

    def mat_peer(dz, dy):
        return lax.rem(z + dz, 4) * 4 + lax.rem(yh + dy, 2) * 2 + core

    def source(j):
        dz, dy = OFFSETS[j]
        return mat_peer((4 - dz) % 4, dy)

    flip = 1 - 2 * core
    other = m + flip
    freq_ids = [freq_peer(*o) for o in OFFSETS]
    mat_ids = [mat_peer(*o) for o in OFFSETS]

    barrier = pltpu.get_barrier_semaphore()
    for o in OFFSETS:
        pl.semaphore_signal(barrier, inc=1, device_id=(freq_peer(*o), m), device_id_type=MESH)
        pl.semaphore_signal(barrier, inc=1, device_id=(f, mat_peer(*o)), device_id_type=MESH)
    pl.semaphore_signal(barrier, inc=1, device_id=(f, other), device_id_type=MESH)

    groups = samples.shape[0]
    per_half = groups // HALVES
    times = traces.shape[0]
    width = traces.shape[2]

    def load(g):
        return pltpu.make_async_copy(
            traces.at[:, pl.ds(pl.multiple_of(g * GROUP, GROUP), GROUP), :],
            samples.at[g],
            load_sem.at[g],
        )

    for g in range(groups):
        load(g).start()
    mat_load = pltpu.make_async_copy(reflection, matrix, mat_sem)

    bands_here = matrix.shape[0]
    owners = partial.shape[1]
    bands = bands_here * owners
    interval = times * owners
    table = jnp.concatenate(table_pair(interval // 16, bands, times, interval), axis=0)
    forward = (table * (1.0 / math.sqrt(interval))).astype(jnp.bfloat16)
    fwd_wide[...] = kron_rows(
        jnp.dot(
            forward, repeat_lanes(times, times * GROUP), preferred_element_type=jnp.float32
        )
    )

    def transform(h):
        def one(i, _):
            g = h * per_half + i
            load(g).wait()
            out = jnp.dot(
                fwd_wide[...],
                samples.at[g].reshape(times * GROUP, width)[...],
                preferred_element_type=jnp.float32,
            )
            out = out.reshape(2, owners, bands_here, GROUP, width).astype(jnp.bfloat16)
            partial[h, :, :, 0, i] = out[0]
            partial[h, :, :, 1, i] = out[1]
            return 0

        lax.fori_loop(0, per_half, one, 0)

    def rs_copy(h, j):
        to = freq_ids[j]
        return pltpu.make_async_remote_copy(
            src_ref=partial.at[h, to], dst_ref=parts.at[h, j],
            send_sem=rs_send.at[h], recv_sem=rs_recv.at[h],
            device_id=(to, m), device_id_type=MESH,
        )

    def rs_all(h):
        return pltpu.make_async_remote_copy(
            src_ref=parts.at[h], dst_ref=parts.at[h],
            send_sem=rs_send.at[h], recv_sem=rs_recv.at[h],
            device_id=(f, other), device_id_type=MESH,
        )

    def ag_copy(h, j):
        relayed = j in RELAYED
        kind = 2 if relayed else int(j != ACROSS)
        return pltpu.make_async_remote_copy(
            src_ref=spectra.at[h, core, (1 + ACROSS) if relayed else 0],
            dst_ref=spectra.at[h, core, 1 + j],
            send_sem=ag_send.at[h, kind], recv_sem=ag_recv.at[h, kind],
            device_id=(f, mat_ids[j - 3] if relayed else mat_ids[j]), device_id_type=MESH,
        )

    def ag_all(h, kind):
        first, count = ((1, 1), (2, 3), (5, 3))[kind]
        part = spectra.at[h, core, pl.ds(first, count)]
        return pltpu.make_async_remote_copy(
            src_ref=part, dst_ref=part,
            send_sem=ag_send.at[h, kind], recv_sem=ag_recv.at[h, kind],
            device_id=(f, other), device_id_type=MESH,
        )

    def core_copy(h, part):
        first, count = ((0, 5), (5, 3))[part]
        held = spectra.at[h, core, pl.ds(first, count)]
        return pltpu.make_async_remote_copy(
            src_ref=held, dst_ref=held,
            send_sem=fw_send.at[h, part], recv_sem=core_recv.at[h, part],
            device_id=(f, other), device_id_type=MESH,
        )

    def br_copy(h, j):
        return pltpu.make_async_remote_copy(
            src_ref=response.at[h], dst_ref=pieces.at[h, f],
            send_sem=br_send.at[h], recv_sem=br_recv.at[h],
            device_id=(freq_ids[j], m), device_id_type=MESH,
        )

    def br_all(h):
        part = pieces.at[h, pl.ds(0, len(OFFSETS))]
        return pltpu.make_async_remote_copy(
            src_ref=part, dst_ref=part,
            send_sem=br_send.at[h], recv_sem=br_recv.at[h],
            device_id=(f, other), device_id_type=MESH,
        )

    peers = range(len(OFFSETS))

    for h in range(HALVES):
        transform(h)
        if h == 0:
            mat_load.start()
            pl.semaphore_wait(barrier, 2 * len(OFFSETS) + 1)
            for j in peers:
                rs_copy(h, j).start()

    inverse = (table * (1.0 / math.sqrt(bands))).astype(jnp.bfloat16)
    inv_wide[...] = kron_rows(
        lax.dot_general(
            inverse,
            repeat_lanes(2 * bands, 2 * bands * GROUP),
            (((0,), (0,)), ((), ())),
            preferred_element_type=jnp.float32,
        )
    )
    inv_copy = pltpu.make_async_copy(inv_wide, inv_out, inv_sem)
    inv_copy.start()

    half_rows = per_half * GROUP
    recv_rows = matrix.shape[2]

    def multiply(h, side, slot):
        block = m if slot == 0 else source(slot - 1)
        block = block + (side - core)
        for k in range(bands_here):
            panel = spectra.at[h, side, slot, k].reshape(2 * half_rows, width)[...]
            cols = pl.ds(pl.multiple_of(block * width, width), width)
            tile = matrix[k, :, :, cols].reshape(2 * recv_rows, width)
            out = lax.dot_general(
                panel, tile, (((1,), (1,)), ((), ())), preferred_element_type=jnp.float32
            )
            if slot == 0 and side is core:
                acc[h, k] = out
            else:
                acc[h, k] += out

    def send_parts(h):
        if h == 0:
            return
        rs_all(h - 1).wait_send()
        for j in peers:
            rs_copy(h, j).start()

    def add_up(h):
        rs_all(h).wait_recv()
        total = partial[h, f].astype(jnp.float32)
        for j in peers:
            total = total + parts[h, j].astype(jnp.float32)
        spectra[h, core, 0] = total.astype(jnp.bfloat16)
        for j in DIRECT:
            ag_copy(h, j).start()

    def relay(h):
        ag_all(h, 0).wait_recv()
        for j in RELAYED:
            ag_copy(h, j).start()

    def first_blocks(h):
        if h == 0:
            mat_load.wait()
        ag_all(h, 1).wait_recv()
        core_copy(h, 0).start()
        for slot in range(5):
            multiply(h, core, slot)

    def last_blocks(h):
        ag_all(h, 2).wait_recv()
        core_copy(h, 1).start()
        for slot in range(5, 8):
            multiply(h, core, slot)
        core_copy(h, 0).wait_recv()
        for slot in range(5):
            multiply(h, 1 - core, slot)
        core_copy(h, 1).wait_recv()
        for slot in range(5, 8):
            multiply(h, 1 - core, slot)
        for k in range(bands_here):
            a = acc[h, k]
            real = a[:half_rows, :recv_rows] - a[half_rows:, recv_rows:]
            imag = a[half_rows:, :recv_rows] + a[:half_rows, recv_rows:]
            response[h, k, 0] = real.reshape(per_half, GROUP, width).astype(jnp.bfloat16)
            response[h, k, 1] = imag.reshape(per_half, GROUP, width).astype(jnp.bfloat16)
        for j in peers:
            br_copy(h, j).start()
        pltpu.make_async_copy(response.at[h], pieces.at[h, f], own_sem.at[h]).start()

    steps = (send_parts, add_up, relay, first_blocks, last_blocks)
    order = sorted(
        (LEAD[i] + h * SPACING / HALVES, i, h) for i in range(len(steps)) for h in range(HALVES)
    )
    for _, i, h in order:
        steps[i](h)

    for h in range(HALVES):
        br_all(h).wait_recv()
        pltpu.make_async_copy(response.at[h], pieces.at[h, f], own_sem.at[h]).wait()
    rs_all(HALVES - 1).wait_send()
    for h in range(HALVES):
        for kind in range(3):
            ag_all(h, kind).wait_send()
        for part in range(2):
            core_copy(h, part).wait_send()
        br_all(h).wait_send()
    inv_copy.wait()


def window_kernel(table, pieces, onset, out, wide, held, left, rows, signal, sems, tab_sem, out_sem):
    times, focal, width = out.shape
    steps = signal.shape[0]
    step = times // steps
    groups = focal // GROUP

    def table_load(i):
        part = pl.ds(i * step * GROUP, step * GROUP)
        return pltpu.make_async_copy(table.at[part], wide.at[part], tab_sem.at[i])

    def store(i):
        return pltpu.make_async_copy(
            signal.at[i], out.at[pl.ds(i * step, step)], out_sem.at[i]
        )

    loads = [pltpu.make_async_copy(pieces.at[h], held.at[h], sems.at[h]) for h in range(HALVES)]
    loads.append(pltpu.make_async_copy(onset, left, sems.at[HALVES]))
    for copy in loads:
        copy.start()
    for i in range(steps):
        table_load(i).start()
    for copy in loads:
        copy.wait()
    per_half = groups // HALVES
    for g in range(groups):
        parts = [
            held[g // per_half, :, :, c, g % per_half]
            .astype(jnp.float32)
            .reshape(wide.shape[1] // 2, width)
            for c in range(2)
        ]
        rows[g] = jnp.concatenate(parts, axis=0).astype(jnp.bfloat16)
    at = lax.axis_index("freq") * times + lax.broadcasted_iota(
        jnp.int32, (step, GROUP, width), 0
    )
    for i in range(steps):
        table_load(i).wait()
        weights = wide[i * step * GROUP : (i + 1) * step * GROUP]
        for g in range(groups):
            value = jnp.dot(weights, rows[g], preferred_element_type=jnp.float32)
            until = left[g * GROUP : (g + 1) * GROUP] - i * step
            kept = jnp.where(at < until[None], value.reshape(step, GROUP, width), 0.0)
            signal[i, :, g * GROUP : (g + 1) * GROUP] = kept.astype(jnp.bfloat16)
        store(i).start()
    for i in range(steps):
        store(i).wait()


def on_device(traces, reflection, onset):
    times, focal, width = traces.shape
    devices = lax.axis_size("freq")
    mats = lax.axis_size("mat")
    per_device = reflection.shape[0]
    bands = per_device * devices
    half = focal // HALVES
    per_half = half // GROUP
    peers = len(OFFSETS)
    bf16 = jnp.bfloat16
    dma = pltpu.SemaphoreType.DMA
    anywhere = pl.BlockSpec(memory_space=pl.ANY)
    pieces, table = pl.pallas_call(
        exchange_kernel,
        out_shape=(
            jax.ShapeDtypeStruct((HALVES, devices, per_device, 2, per_half, GROUP, width), bf16),
            jax.ShapeDtypeStruct((times * GROUP, 2 * bands * GROUP), bf16),
        ),
        in_specs=[anywhere, anywhere],
        out_specs=(anywhere, anywhere),
        scratch_shapes=[
            pltpu.VMEM((focal // GROUP, times, GROUP, width), bf16),
            pltpu.VMEM(reflection.shape, bf16),
            pltpu.VMEM((2 * bands * GROUP, times * GROUP), bf16),
            pltpu.VMEM((times * GROUP, 2 * bands * GROUP), bf16),
            pltpu.VMEM((HALVES, devices, per_device, 2, per_half, GROUP, width), bf16),
            pltpu.VMEM((HALVES, peers, per_device, 2, per_half, GROUP, width), bf16),
            pltpu.VMEM((HALVES, 2, mats // 2, per_device, 2, per_half, GROUP, width), bf16),
            pltpu.VMEM((HALVES, per_device, 2 * half, 2 * width), jnp.float32),
            pltpu.VMEM((HALVES, per_device, 2, per_half, GROUP, width), bf16),
            dma((focal // GROUP,)),
            dma,
            dma,
            dma((HALVES,)),
            dma((HALVES,)),
            dma((HALVES,)),
            dma((HALVES, 3)),
            dma((HALVES, 3)),
            dma((HALVES, 2)),
            dma((HALVES, 2)),
            dma((HALVES,)),
            dma((HALVES,)),
        ],
        compiler_params=pltpu.CompilerParams(
            collective_id=0, has_side_effects=True, vmem_limit_bytes=60 * 2**20
        ),
        name="exchange",
    )(traces, reflection)
    return pl.pallas_call(
        window_kernel,
        out_shape=jax.ShapeDtypeStruct((times, focal, width), bf16),
        in_specs=[anywhere, anywhere, anywhere],
        out_specs=anywhere,
        scratch_shapes=[
            pltpu.VMEM(table.shape, bf16),
            pltpu.VMEM(pieces.shape, bf16),
            pltpu.VMEM(onset.shape, jnp.int32),
            pltpu.VMEM((focal // GROUP, table.shape[1], width), bf16),
            pltpu.VMEM((STEPS, times // STEPS, focal, width), bf16),
            dma((HALVES + 1,)),
            dma((STEPS,)),
            dma((STEPS,)),
        ],
        compiler_params=pltpu.CompilerParams(vmem_limit_bytes=60 * 2**20),
        name="window",
    )(table, pieces, onset)


def solution(mesh):
    placed = (P("freq", None, "mat"), P("freq", None, "mat", None), P(None, "mat"))
    return jax.shard_map(
        on_device, mesh=mesh, in_specs=placed, out_specs=P("freq", None, "mat"), check_vma=False
    )
```

```python
import math

import jax
import jax.numpy as jnp
from jax import lax
from jax.experimental import pallas as pl
from jax.experimental.pallas import tpu as pltpu
from jax.sharding import PartitionSpec as P

MESH = pl.DeviceIdType.MESH
HALVES = 4
GROUP = 8
STEPS = 4
LEAD, SPACING = (-4.5, 0.0, 3.8, 5.0, 8.0), 9.6
OFFSETS = ((0, 1), (1, 0), (3, 0), (2, 0), (1, 1), (3, 1), (2, 1))
FREQ_OFFSETS = ((0, 1), (1, 1), (3, 1), (2, 1), (1, 0), (3, 0), (2, 0))
ACROSS, DIRECT, RELAYED = 0, (0, 1, 2, 3), (4, 5, 6)


def table_pair(first, bands, times, interval):
    k = first + lax.broadcasted_iota(jnp.int32, (bands, times), 0)
    t = lax.axis_index("freq") * times + lax.broadcasted_iota(jnp.int32, (bands, times), 1)
    angles = ((k * t) & (interval - 1)).astype(jnp.float32) * (2.0 * math.pi / interval)
    return jnp.cos(angles), -jnp.sin(angles)


def kron_rows(wide):
    rows, lanes = wide.shape
    sub = lax.broadcasted_iota(jnp.int32, (1, GROUP, lanes), 1)
    lane = lax.broadcasted_iota(jnp.int32, (1, GROUP, lanes), 2) & (GROUP - 1)
    full = jnp.where(sub == lane, wide[:, None, :], 0.0)
    return full.reshape(rows * GROUP, lanes).astype(jnp.bfloat16)


def repeat_lanes(inner, lanes):
    col = lax.broadcasted_iota(jnp.int32, (inner, lanes), 1) >> 3
    row = lax.broadcasted_iota(jnp.int32, (inner, lanes), 0)
    return jnp.where(col == row, 1.0, 0.0).astype(jnp.bfloat16)


def exchange_kernel(
    traces, reflection, pieces, inv_out,
    samples, matrix, fwd_wide, inv_wide, partial, parts, spectra, acc, response,
    load_sem, mat_sem, inv_sem, own_sem,
    rs_send, rs_recv, ag_send, ag_recv, fw_send, core_recv, br_send, br_recv,
):
    f = lax.axis_index("freq")
    m = lax.axis_index("mat")
    x, yl = f // 2, f % 2
    z, yh, core = m // 4, (m // 2) % 2, m % 2

    def freq_peer(dx, dy):
        return lax.rem(x + dx, 4) * 2 + lax.rem(yl + dy, 2)

    def mat_peer(dz, dy):
        return lax.rem(z + dz, 4) * 4 + lax.rem(yh + dy, 2) * 2 + core

    def source(j):
        dz, dy = OFFSETS[j]
        return mat_peer((4 - dz) % 4, dy)

    flip = 1 - 2 * core
    other = m + flip
    freq_ids = [freq_peer(*o) for o in FREQ_OFFSETS]
    mat_ids = [mat_peer(*o) for o in OFFSETS]

    barrier = pltpu.get_barrier_semaphore()
    for o in OFFSETS:
        pl.semaphore_signal(barrier, inc=1, device_id=(freq_peer(*o), m), device_id_type=MESH)
        pl.semaphore_signal(barrier, inc=1, device_id=(f, mat_peer(*o)), device_id_type=MESH)
    pl.semaphore_signal(barrier, inc=1, device_id=(f, other), device_id_type=MESH)

    groups = samples.shape[0]
    per_half = groups // HALVES
    times = traces.shape[0]
    width = traces.shape[2]

    def load(g):
        return pltpu.make_async_copy(
            traces.at[:, pl.ds(pl.multiple_of(g * GROUP, GROUP), GROUP), :],
            samples.at[g],
            load_sem.at[g],
        )

    for g in range(groups):
        load(g).start()
    mat_load = pltpu.make_async_copy(reflection, matrix, mat_sem)

    bands_here = matrix.shape[0]
    owners = partial.shape[1]
    bands = bands_here * owners
    interval = times * owners
    table = jnp.concatenate(table_pair(interval // 16, bands, times, interval), axis=0)
    forward = (table * (1.0 / math.sqrt(interval))).astype(jnp.bfloat16)
    fwd_wide[...] = kron_rows(
        jnp.dot(
            forward, repeat_lanes(times, times * GROUP), preferred_element_type=jnp.float32
        )
    )

    def transform(h):
        def one(i, _):
            g = h * per_half + i
            load(g).wait()
            out = jnp.dot(
                fwd_wide[...],
                samples.at[g].reshape(times * GROUP, width)[...],
                preferred_element_type=jnp.float32,
            )
            out = out.reshape(2, owners, bands_here, GROUP, width).astype(jnp.bfloat16)
            partial[h, :, :, 0, i] = out[0]
            partial[h, :, :, 1, i] = out[1]
            return 0

        lax.fori_loop(0, per_half, one, 0)

    def rs_copy(h, j):
        to = freq_ids[j]
        return pltpu.make_async_remote_copy(
            src_ref=partial.at[h, to], dst_ref=parts.at[h, j],
            send_sem=rs_send.at[h], recv_sem=rs_recv.at[h],
            device_id=(to, m), device_id_type=MESH,
        )

    def rs_all(h):
        return pltpu.make_async_remote_copy(
            src_ref=parts.at[h], dst_ref=parts.at[h],
            send_sem=rs_send.at[h], recv_sem=rs_recv.at[h],
            device_id=(f, other), device_id_type=MESH,
        )

    def ag_copy(h, j):
        relayed = j in RELAYED
        kind = 2 if relayed else int(j != ACROSS)
        return pltpu.make_async_remote_copy(
            src_ref=spectra.at[h, core, (1 + ACROSS) if relayed else 0],
            dst_ref=spectra.at[h, core, 1 + j],
            send_sem=ag_send.at[h, kind], recv_sem=ag_recv.at[h, kind],
            device_id=(f, mat_ids[j - 3] if relayed else mat_ids[j]), device_id_type=MESH,
        )

    def ag_all(h, kind):
        first, count = ((1, 1), (2, 3), (5, 3))[kind]
        part = spectra.at[h, core, pl.ds(first, count)]
        return pltpu.make_async_remote_copy(
            src_ref=part, dst_ref=part,
            send_sem=ag_send.at[h, kind], recv_sem=ag_recv.at[h, kind],
            device_id=(f, other), device_id_type=MESH,
        )

    def core_copy(h, part):
        first, count = ((0, 5), (5, 3))[part]
        held = spectra.at[h, core, pl.ds(first, count)]
        return pltpu.make_async_remote_copy(
            src_ref=held, dst_ref=held,
            send_sem=fw_send.at[h, part], recv_sem=core_recv.at[h, part],
            device_id=(f, other), device_id_type=MESH,
        )

    def br_copy(h, j):
        return pltpu.make_async_remote_copy(
            src_ref=response.at[h], dst_ref=pieces.at[h, f],
            send_sem=br_send.at[h], recv_sem=br_recv.at[h],
            device_id=(freq_ids[j], m), device_id_type=MESH,
        )

    def br_all(h):
        part = pieces.at[h, pl.ds(0, len(OFFSETS))]
        return pltpu.make_async_remote_copy(
            src_ref=part, dst_ref=part,
            send_sem=br_send.at[h], recv_sem=br_recv.at[h],
            device_id=(f, other), device_id_type=MESH,
        )

    peers = range(len(OFFSETS))

    for h in range(HALVES):
        transform(h)
        if h == 0:
            mat_load.start()
            pl.semaphore_wait(barrier, 2 * len(OFFSETS) + 1)
            for j in peers:
                rs_copy(h, j).start()

    inverse = (table * (1.0 / math.sqrt(bands))).astype(jnp.bfloat16)
    inv_wide[...] = kron_rows(
        lax.dot_general(
            inverse,
            repeat_lanes(2 * bands, 2 * bands * GROUP),
            (((0,), (0,)), ((), ())),
            preferred_element_type=jnp.float32,
        )
    )
    inv_copy = pltpu.make_async_copy(inv_wide, inv_out, inv_sem)
    inv_copy.start()

    half_rows = per_half * GROUP
    recv_rows = matrix.shape[2]

    def multiply(h, side, slot):
        block = m if slot == 0 else source(slot - 1)
        block = block + (side - core)
        for k in range(bands_here):
            panel = spectra.at[h, side, slot, k].reshape(2 * half_rows, width)[...]
            cols = pl.ds(pl.multiple_of(block * width, width), width)
            tile = matrix[k, :, :, cols].reshape(2 * recv_rows, width)
            out = lax.dot_general(
                panel, tile, (((1,), (1,)), ((), ())), preferred_element_type=jnp.float32
            )
            if slot == 0 and side is core:
                acc[h, k] = out
            else:
                acc[h, k] += out

    def send_parts(h):
        if h == 0:
            return
        rs_all(h - 1).wait_send()
        for j in peers:
            rs_copy(h, j).start()

    def add_up(h):
        rs_all(h).wait_recv()
        total = partial[h, f].astype(jnp.float32)
        for j in peers:
            total = total + parts[h, j].astype(jnp.float32)
        spectra[h, core, 0] = total.astype(jnp.bfloat16)
        for j in DIRECT:
            ag_copy(h, j).start()

    def relay(h):
        ag_all(h, 0).wait_recv()
        for j in RELAYED:
            ag_copy(h, j).start()

    def first_blocks(h):
        if h == 0:
            mat_load.wait()
        ag_all(h, 1).wait_recv()
        core_copy(h, 0).start()
        for slot in range(5):
            multiply(h, core, slot)

    def last_blocks(h):
        ag_all(h, 2).wait_recv()
        core_copy(h, 1).start()
        for slot in range(5, 8):
            multiply(h, core, slot)
        core_copy(h, 0).wait_recv()
        for slot in range(5):
            multiply(h, 1 - core, slot)
        core_copy(h, 1).wait_recv()
        for slot in range(5, 8):
            multiply(h, 1 - core, slot)
        for k in range(bands_here):
            a = acc[h, k]
            real = a[:half_rows, :recv_rows] - a[half_rows:, recv_rows:]
            imag = a[half_rows:, :recv_rows] + a[:half_rows, recv_rows:]
            response[h, k, 0] = real.reshape(per_half, GROUP, width).astype(jnp.bfloat16)
            response[h, k, 1] = imag.reshape(per_half, GROUP, width).astype(jnp.bfloat16)
        if h:
            br_all(h - 1).wait_send()
        for j in peers:
            br_copy(h, j).start()
        pltpu.make_async_copy(response.at[h], pieces.at[h, f], own_sem.at[h]).start()

    steps = (send_parts, add_up, relay, first_blocks, last_blocks)
    order = sorted(
        (LEAD[i] + h * SPACING / HALVES, i, h) for i in range(len(steps)) for h in range(HALVES)
    )
    for _, i, h in order:
        steps[i](h)

    for h in range(HALVES):
        br_all(h).wait_recv()
        pltpu.make_async_copy(response.at[h], pieces.at[h, f], own_sem.at[h]).wait()
    rs_all(HALVES - 1).wait_send()
    for h in range(HALVES):
        for kind in range(3):
            ag_all(h, kind).wait_send()
        for part in range(2):
            core_copy(h, part).wait_send()
    br_all(HALVES - 1).wait_send()
    inv_copy.wait()


def window_kernel(table, pieces, onset, out, wide, held, left, rows, signal, sems, tab_sem, out_sem):
    times, focal, width = out.shape
    steps = signal.shape[0]
    step = times // steps
    groups = focal // GROUP

    def table_load(i):
        part = pl.ds(i * step * GROUP, step * GROUP)
        return pltpu.make_async_copy(table.at[part], wide.at[part], tab_sem.at[i])

    def store(i):
        return pltpu.make_async_copy(
            signal.at[i], out.at[pl.ds(i * step, step)], out_sem.at[i]
        )

    loads = [pltpu.make_async_copy(pieces.at[h], held.at[h], sems.at[h]) for h in range(HALVES)]
    loads.append(pltpu.make_async_copy(onset, left, sems.at[HALVES]))
    for copy in loads:
        copy.start()
    for i in range(steps):
        table_load(i).start()
    for copy in loads:
        copy.wait()
    per_half = groups // HALVES
    for g in range(groups):
        parts = [
            held[g // per_half, :, :, c, g % per_half]
            .astype(jnp.float32)
            .reshape(wide.shape[1] // 2, width)
            for c in range(2)
        ]
        rows[g] = jnp.concatenate(parts, axis=0).astype(jnp.bfloat16)
    at = lax.axis_index("freq") * times + lax.broadcasted_iota(
        jnp.int32, (step, GROUP, width), 0
    )
    for i in range(steps):
        table_load(i).wait()
        weights = wide[i * step * GROUP : (i + 1) * step * GROUP]
        for g in range(groups):
            value = jnp.dot(weights, rows[g], preferred_element_type=jnp.float32)
            until = left[g * GROUP : (g + 1) * GROUP] - i * step
            kept = jnp.where(at < until[None], value.reshape(step, GROUP, width), 0.0)
            signal[i, :, g * GROUP : (g + 1) * GROUP] = kept.astype(jnp.bfloat16)
        store(i).start()
    for i in range(steps):
        store(i).wait()


def on_device(traces, reflection, onset):
    times, focal, width = traces.shape
    devices = lax.axis_size("freq")
    mats = lax.axis_size("mat")
    per_device = reflection.shape[0]
    bands = per_device * devices
    half = focal // HALVES
    per_half = half // GROUP
    peers = len(OFFSETS)
    bf16 = jnp.bfloat16
    dma = pltpu.SemaphoreType.DMA
    anywhere = pl.BlockSpec(memory_space=pl.ANY)
    pieces, table = pl.pallas_call(
        exchange_kernel,
        out_shape=(
            jax.ShapeDtypeStruct((HALVES, devices, per_device, 2, per_half, GROUP, width), bf16),
            jax.ShapeDtypeStruct((times * GROUP, 2 * bands * GROUP), bf16),
        ),
        in_specs=[anywhere, anywhere],
        out_specs=(anywhere, anywhere),
        scratch_shapes=[
            pltpu.VMEM((focal // GROUP, times, GROUP, width), bf16),
            pltpu.VMEM(reflection.shape, bf16),
            pltpu.VMEM((2 * bands * GROUP, times * GROUP), bf16),
            pltpu.VMEM((times * GROUP, 2 * bands * GROUP), bf16),
            pltpu.VMEM((HALVES, devices, per_device, 2, per_half, GROUP, width), bf16),
            pltpu.VMEM((HALVES, peers, per_device, 2, per_half, GROUP, width), bf16),
            pltpu.VMEM((HALVES, 2, mats // 2, per_device, 2, per_half, GROUP, width), bf16),
            pltpu.VMEM((HALVES, per_device, 2 * half, 2 * width), jnp.float32),
            pltpu.VMEM((HALVES, per_device, 2, per_half, GROUP, width), bf16),
            dma((focal // GROUP,)),
            dma,
            dma,
            dma((HALVES,)),
            dma((HALVES,)),
            dma((HALVES,)),
            dma((HALVES, 3)),
            dma((HALVES, 3)),
            dma((HALVES, 2)),
            dma((HALVES, 2)),
            dma((HALVES,)),
            dma((HALVES,)),
        ],
        compiler_params=pltpu.CompilerParams(
            collective_id=0, has_side_effects=True, vmem_limit_bytes=60 * 2**20
        ),
        name="exchange",
    )(traces, reflection)
    return pl.pallas_call(
        window_kernel,
        out_shape=jax.ShapeDtypeStruct((times, focal, width), bf16),
        in_specs=[anywhere, anywhere, anywhere],
        out_specs=anywhere,
        scratch_shapes=[
            pltpu.VMEM(table.shape, bf16),
            pltpu.VMEM(pieces.shape, bf16),
            pltpu.VMEM(onset.shape, jnp.int32),
            pltpu.VMEM((focal // GROUP, table.shape[1], width), bf16),
            pltpu.VMEM((STEPS, times // STEPS, focal, width), bf16),
            dma((HALVES + 1,)),
            dma((STEPS,)),
            dma((STEPS,)),
        ],
        compiler_params=pltpu.CompilerParams(vmem_limit_bytes=60 * 2**20),
        name="window",
    )(table, pieces, onset)


def solution(mesh):
    placed = (P("freq", None, "mat"), P("freq", None, "mat", None), P(None, "mat"))
    return jax.shard_map(
        on_device, mesh=mesh, in_specs=placed, out_specs=P("freq", None, "mat"), check_vma=False
    )
```

```python
import math

import jax
import jax.numpy as jnp
from jax import lax
from jax.experimental import pallas as pl
from jax.experimental.pallas import tpu as pltpu
from jax.sharding import PartitionSpec as P

MESH = pl.DeviceIdType.MESH
HALVES = 4
GROUP = 8
STEPS = 2
LEAD, SPACING = (-4.5, 0.0, 3.8, 5.0, 8.0), 9.6
OFFSETS = ((0, 1), (1, 0), (3, 0), (2, 0), (1, 1), (3, 1), (2, 1))
FREQ_OFFSETS = ((0, 1), (1, 1), (3, 1), (2, 1), (1, 0), (3, 0), (2, 0))
ACROSS, DIRECT, RELAYED = 0, (0, 1, 2, 3), (4, 5, 6)


def table_pair(first, bands, times, interval):
    k = first + lax.broadcasted_iota(jnp.int32, (bands, times), 0)
    t = lax.axis_index("freq") * times + lax.broadcasted_iota(jnp.int32, (bands, times), 1)
    angles = ((k * t) & (interval - 1)).astype(jnp.float32) * (2.0 * math.pi / interval)
    return jnp.cos(angles), -jnp.sin(angles)


def kron_rows(wide):
    rows, lanes = wide.shape
    sub = lax.broadcasted_iota(jnp.int32, (1, GROUP, lanes), 1)
    lane = lax.broadcasted_iota(jnp.int32, (1, GROUP, lanes), 2) & (GROUP - 1)
    full = jnp.where(sub == lane, wide[:, None, :], 0.0)
    return full.reshape(rows * GROUP, lanes).astype(jnp.bfloat16)


def repeat_lanes(inner, lanes):
    col = lax.broadcasted_iota(jnp.int32, (inner, lanes), 1) >> 3
    row = lax.broadcasted_iota(jnp.int32, (inner, lanes), 0)
    return jnp.where(col == row, 1.0, 0.0).astype(jnp.bfloat16)


def exchange_kernel(
    traces, reflection, pieces, inv_out,
    samples, matrix, fwd_wide, inv_wide, partial, parts, spectra, acc, response,
    load_sem, mat_sem, inv_sem, own_sem,
    rs_send, rs_recv, ag_send, ag_recv, fw_send, core_recv, br_send, br_recv,
):
    f = lax.axis_index("freq")
    m = lax.axis_index("mat")
    x, yl = f // 2, f % 2
    z, yh, core = m // 4, (m // 2) % 2, m % 2

    def freq_peer(dx, dy):
        return lax.rem(x + dx, 4) * 2 + lax.rem(yl + dy, 2)

    def mat_peer(dz, dy):
        return lax.rem(z + dz, 4) * 4 + lax.rem(yh + dy, 2) * 2 + core

    def source(j):
        dz, dy = OFFSETS[j]
        return mat_peer((4 - dz) % 4, dy)

    flip = 1 - 2 * core
    other = m + flip
    freq_ids = [freq_peer(*o) for o in FREQ_OFFSETS]
    mat_ids = [mat_peer(*o) for o in OFFSETS]

    barrier = pltpu.get_barrier_semaphore()
    for o in OFFSETS:
        pl.semaphore_signal(barrier, inc=1, device_id=(freq_peer(*o), m), device_id_type=MESH)
        pl.semaphore_signal(barrier, inc=1, device_id=(f, mat_peer(*o)), device_id_type=MESH)
    pl.semaphore_signal(barrier, inc=1, device_id=(f, other), device_id_type=MESH)

    groups = samples.shape[0]
    per_half = groups // HALVES
    times = traces.shape[0]
    width = traces.shape[2]

    def load(g):
        return pltpu.make_async_copy(
            traces.at[:, pl.ds(pl.multiple_of(g * GROUP, GROUP), GROUP), :],
            samples.at[g],
            load_sem.at[g],
        )

    for g in range(groups):
        load(g).start()
    mat_load = pltpu.make_async_copy(reflection, matrix, mat_sem)

    bands_here = matrix.shape[0]
    owners = partial.shape[1]
    bands = bands_here * owners
    interval = times * owners
    table = jnp.concatenate(table_pair(interval // 16, bands, times, interval), axis=0)
    forward = (table * (1.0 / math.sqrt(interval))).astype(jnp.bfloat16)
    fwd_wide[...] = kron_rows(
        jnp.dot(
            forward, repeat_lanes(times, times * GROUP), preferred_element_type=jnp.float32
        )
    )

    def transform(h):
        def one(i, _):
            g = h * per_half + i
            load(g).wait()
            out = jnp.dot(
                fwd_wide[...],
                samples.at[g].reshape(times * GROUP, width)[...],
                preferred_element_type=jnp.float32,
            )
            out = out.reshape(2, owners, bands_here, GROUP, width).astype(jnp.bfloat16)
            partial[h, :, :, 0, i] = out[0]
            partial[h, :, :, 1, i] = out[1]
            return 0

        lax.fori_loop(0, per_half, one, 0)

    def rs_copy(h, j):
        to = freq_ids[j]
        return pltpu.make_async_remote_copy(
            src_ref=partial.at[h, to], dst_ref=parts.at[h, j],
            send_sem=rs_send.at[h], recv_sem=rs_recv.at[h],
            device_id=(to, m), device_id_type=MESH,
        )

    def rs_all(h):
        return pltpu.make_async_remote_copy(
            src_ref=parts.at[h], dst_ref=parts.at[h],
            send_sem=rs_send.at[h], recv_sem=rs_recv.at[h],
            device_id=(f, other), device_id_type=MESH,
        )

    def ag_copy(h, j):
        relayed = j in RELAYED
        kind = 2 if relayed else int(j != ACROSS)
        return pltpu.make_async_remote_copy(
            src_ref=spectra.at[h, core, (1 + ACROSS) if relayed else 0],
            dst_ref=spectra.at[h, core, 1 + j],
            send_sem=ag_send.at[h, kind], recv_sem=ag_recv.at[h, kind],
            device_id=(f, mat_ids[j - 3] if relayed else mat_ids[j]), device_id_type=MESH,
        )

    def ag_all(h, kind):
        first, count = ((1, 1), (2, 3), (5, 3))[kind]
        part = spectra.at[h, core, pl.ds(first, count)]
        return pltpu.make_async_remote_copy(
            src_ref=part, dst_ref=part,
            send_sem=ag_send.at[h, kind], recv_sem=ag_recv.at[h, kind],
            device_id=(f, other), device_id_type=MESH,
        )

    def core_copy(h, part):
        first, count = ((0, 5), (5, 3))[part]
        held = spectra.at[h, core, pl.ds(first, count)]
        return pltpu.make_async_remote_copy(
            src_ref=held, dst_ref=held,
            send_sem=fw_send.at[h, part], recv_sem=core_recv.at[h, part],
            device_id=(f, other), device_id_type=MESH,
        )

    def br_copy(h, j):
        return pltpu.make_async_remote_copy(
            src_ref=response.at[h], dst_ref=pieces.at[h, f],
            send_sem=br_send.at[h], recv_sem=br_recv.at[h],
            device_id=(freq_ids[j], m), device_id_type=MESH,
        )

    def br_all(h):
        part = pieces.at[h, pl.ds(0, len(OFFSETS))]
        return pltpu.make_async_remote_copy(
            src_ref=part, dst_ref=part,
            send_sem=br_send.at[h], recv_sem=br_recv.at[h],
            device_id=(f, other), device_id_type=MESH,
        )

    peers = range(len(OFFSETS))

    for h in range(HALVES):
        transform(h)
        if h == 0:
            mat_load.start()
            pl.semaphore_wait(barrier, 2 * len(OFFSETS) + 1)
            for j in peers:
                rs_copy(h, j).start()

    inverse = (table * (1.0 / math.sqrt(bands))).astype(jnp.bfloat16)
    inv_wide[...] = kron_rows(
        lax.dot_general(
            inverse,
            repeat_lanes(2 * bands, 2 * bands * GROUP),
            (((0,), (0,)), ((), ())),
            preferred_element_type=jnp.float32,
        )
    )
    inv_copy = pltpu.make_async_copy(inv_wide, inv_out, inv_sem)
    inv_copy.start()

    half_rows = per_half * GROUP
    recv_rows = matrix.shape[2]

    def multiply(h, side, slot):
        block = m if slot == 0 else source(slot - 1)
        block = block + (side - core)
        for k in range(bands_here):
            panel = spectra.at[h, side, slot, k].reshape(2 * half_rows, width)[...]
            cols = pl.ds(pl.multiple_of(block * width, width), width)
            tile = matrix[k, :, :, cols].reshape(2 * recv_rows, width)
            out = lax.dot_general(
                panel, tile, (((1,), (1,)), ((), ())), preferred_element_type=jnp.float32
            )
            if slot == 0 and side is core:
                acc[h, k] = out
            else:
                acc[h, k] += out

    def send_parts(h):
        if h == 0:
            return
        rs_all(h - 1).wait_send()
        for j in peers:
            rs_copy(h, j).start()

    def add_up(h):
        rs_all(h).wait_recv()
        total = partial[h, f].astype(jnp.float32)
        for j in peers:
            total = total + parts[h, j].astype(jnp.float32)
        spectra[h, core, 0] = total.astype(jnp.bfloat16)
        for j in DIRECT:
            ag_copy(h, j).start()

    def relay(h):
        ag_all(h, 0).wait_recv()
        for j in RELAYED:
            ag_copy(h, j).start()

    def first_blocks(h):
        if h == 0:
            mat_load.wait()
        ag_all(h, 1).wait_recv()
        core_copy(h, 0).start()
        for slot in range(5):
            multiply(h, core, slot)

    def last_blocks(h):
        ag_all(h, 2).wait_recv()
        core_copy(h, 1).start()
        for slot in range(5, 8):
            multiply(h, core, slot)
        core_copy(h, 0).wait_recv()
        for slot in range(5):
            multiply(h, 1 - core, slot)
        core_copy(h, 1).wait_recv()
        for slot in range(5, 8):
            multiply(h, 1 - core, slot)
        for k in range(bands_here):
            a = acc[h, k]
            real = a[:half_rows, :recv_rows] - a[half_rows:, recv_rows:]
            imag = a[half_rows:, :recv_rows] + a[:half_rows, recv_rows:]
            response[h, k, 0] = real.reshape(per_half, GROUP, width).astype(jnp.bfloat16)
            response[h, k, 1] = imag.reshape(per_half, GROUP, width).astype(jnp.bfloat16)
        if h:
            br_all(h - 1).wait_send()
        for j in peers:
            br_copy(h, j).start()
        pltpu.make_async_copy(response.at[h], pieces.at[h, f], own_sem.at[h]).start()

    steps = (send_parts, add_up, relay, first_blocks, last_blocks)
    order = sorted(
        (LEAD[i] + h * SPACING / HALVES, i, h) for i in range(len(steps)) for h in range(HALVES)
    )
    for _, i, h in order:
        steps[i](h)

    for h in range(HALVES):
        br_all(h).wait_recv()
        pltpu.make_async_copy(response.at[h], pieces.at[h, f], own_sem.at[h]).wait()
    rs_all(HALVES - 1).wait_send()
    for h in range(HALVES):
        for kind in range(3):
            ag_all(h, kind).wait_send()
        for part in range(2):
            core_copy(h, part).wait_send()
    br_all(HALVES - 1).wait_send()
    inv_copy.wait()


def window_kernel(table, pieces, onset, out, wide, held, left, rows, signal, sems, tab_sem, out_sem):
    times, focal, width = out.shape
    steps = signal.shape[0]
    step = times // steps
    groups = focal // GROUP

    def table_load(i):
        part = pl.ds(i * step * GROUP, step * GROUP)
        return pltpu.make_async_copy(table.at[part], wide.at[part], tab_sem.at[i])

    def store(i):
        return pltpu.make_async_copy(
            signal.at[i], out.at[pl.ds(i * step, step)], out_sem.at[i]
        )

    loads = [pltpu.make_async_copy(pieces.at[h], held.at[h], sems.at[h]) for h in range(HALVES)]
    loads.append(pltpu.make_async_copy(onset, left, sems.at[HALVES]))
    for copy in loads:
        copy.start()
    for i in range(steps):
        table_load(i).start()
    for copy in loads:
        copy.wait()
    per_half = groups // HALVES
    for g in range(groups):
        parts = [
            held[g // per_half, :, :, c, g % per_half]
            .astype(jnp.float32)
            .reshape(wide.shape[1] // 2, width)
            for c in range(2)
        ]
        rows[g] = jnp.concatenate(parts, axis=0).astype(jnp.bfloat16)
    at = lax.axis_index("freq") * times + lax.broadcasted_iota(
        jnp.int32, (step, GROUP, width), 0
    )
    for i in range(steps):
        table_load(i).wait()
        weights = wide[i * step * GROUP : (i + 1) * step * GROUP]
        for g in range(groups):
            value = jnp.dot(weights, rows[g], preferred_element_type=jnp.float32)
            until = left[g * GROUP : (g + 1) * GROUP] - i * step
            kept = jnp.where(at < until[None], value.reshape(step, GROUP, width), 0.0)
            signal[i, :, g * GROUP : (g + 1) * GROUP] = kept.astype(jnp.bfloat16)
        store(i).start()
    for i in range(steps):
        store(i).wait()


def on_device(traces, reflection, onset):
    times, focal, width = traces.shape
    devices = lax.axis_size("freq")
    mats = lax.axis_size("mat")
    per_device = reflection.shape[0]
    bands = per_device * devices
    half = focal // HALVES
    per_half = half // GROUP
    peers = len(OFFSETS)
    bf16 = jnp.bfloat16
    dma = pltpu.SemaphoreType.DMA
    anywhere = pl.BlockSpec(memory_space=pl.ANY)
    pieces, table = pl.pallas_call(
        exchange_kernel,
        out_shape=(
            jax.ShapeDtypeStruct((HALVES, devices, per_device, 2, per_half, GROUP, width), bf16),
            jax.ShapeDtypeStruct((times * GROUP, 2 * bands * GROUP), bf16),
        ),
        in_specs=[anywhere, anywhere],
        out_specs=(anywhere, anywhere),
        scratch_shapes=[
            pltpu.VMEM((focal // GROUP, times, GROUP, width), bf16),
            pltpu.VMEM(reflection.shape, bf16),
            pltpu.VMEM((2 * bands * GROUP, times * GROUP), bf16),
            pltpu.VMEM((times * GROUP, 2 * bands * GROUP), bf16),
            pltpu.VMEM((HALVES, devices, per_device, 2, per_half, GROUP, width), bf16),
            pltpu.VMEM((HALVES, peers, per_device, 2, per_half, GROUP, width), bf16),
            pltpu.VMEM((HALVES, 2, mats // 2, per_device, 2, per_half, GROUP, width), bf16),
            pltpu.VMEM((HALVES, per_device, 2 * half, 2 * width), jnp.float32),
            pltpu.VMEM((HALVES, per_device, 2, per_half, GROUP, width), bf16),
            dma((focal // GROUP,)),
            dma,
            dma,
            dma((HALVES,)),
            dma((HALVES,)),
            dma((HALVES,)),
            dma((HALVES, 3)),
            dma((HALVES, 3)),
            dma((HALVES, 2)),
            dma((HALVES, 2)),
            dma((HALVES,)),
            dma((HALVES,)),
        ],
        compiler_params=pltpu.CompilerParams(
            collective_id=0, has_side_effects=True, vmem_limit_bytes=60 * 2**20
        ),
        name="exchange",
    )(traces, reflection)
    return pl.pallas_call(
        window_kernel,
        out_shape=jax.ShapeDtypeStruct((times, focal, width), bf16),
        in_specs=[anywhere, anywhere, anywhere],
        out_specs=anywhere,
        scratch_shapes=[
            pltpu.VMEM(table.shape, bf16),
            pltpu.VMEM(pieces.shape, bf16),
            pltpu.VMEM(onset.shape, jnp.int32),
            pltpu.VMEM((focal // GROUP, table.shape[1], width), bf16),
            pltpu.VMEM((STEPS, times // STEPS, focal, width), bf16),
            dma((HALVES + 1,)),
            dma((STEPS,)),
            dma((STEPS,)),
        ],
        compiler_params=pltpu.CompilerParams(vmem_limit_bytes=60 * 2**20),
        name="window",
    )(table, pieces, onset)


def solution(mesh):
    placed = (P("freq", None, "mat"), P("freq", None, "mat", None), P(None, "mat"))
    return jax.shard_map(
        on_device, mesh=mesh, in_specs=placed, out_specs=P("freq", None, "mat"), check_vma=False
    )
```
